32 devices in a mesh: dp: 4 (over x, core), context: 4 (over z), tensor: 2 (over y).
Axes of the slice: x: 2, y: 2, z: 4, core: 2. Of those that a mesh axis runs over, the one named last changes fastest.
Arguments:
- tokens: bfloat16 [4, 4096, 768], P('dp', 'context'), may hold values from -6 to 6
- positions: int32 [4, 4096], P('dp', 'context'), may hold values from 0 to 4095, each once within a row
- first_gain: float32 [768], replicated, may hold values from 0.5 to 1.5
- first_shift: float32 [768], replicated, may hold values from -3 to 3
- second_gain: float32 [768], replicated, may hold values from 0.5 to 1.5
- second_shift: float32 [768], replicated, may hold values from -3 to 3
- w_query: bfloat16 [768, 768], P('dp', 'tensor'), may hold values from -0.21875 to 0.21875
- w_key: bfloat16 [768, 768], P('dp', 'tensor'), may hold values from -0.21875 to 0.21875
- w_value: bfloat16 [768, 768], P('dp', 'tensor'), may hold values from -0.21875 to 0.21875
- query_bias: float32 [768], P('tensor'), may hold values from -3 to 3
- key_bias: float32 [768], P('tensor'), may hold values from -3 to 3
- value_bias: float32 [768], P('tensor'), may hold values from -3 to 3
- w_out: bfloat16 [768, 768], P('tensor', 'dp'), may hold values from -0.875 to 0.875
- out_bias: float32 [768], replicated, may hold values from -3 to 3
- w_up: bfloat16 [768, 3072], P('dp', 'tensor'), may hold values from -0.21875 to 0.21875
- up_bias: float32 [3072], P('tensor'), may hold values from -3 to 3
- w_down: bfloat16 [3072, 768], P('tensor', 'dp'), may hold values from -0.109375 to 0.109375
- down_bias: float32 [768], replicated, may hold values from -3 to 3
- cotangent: bfloat16 [4, 4096, 768], P('dp', 'context'), may hold values from -6 to 6
Outputs:
- block_out: bfloat16 [4, 4096, 768], P('dp', 'context')
- grad_tokens: float32 [4, 4096, 768], P('dp', 'context')
- grad_first_gain: float32 [768], replicated
- grad_first_shift: float32 [768], replicated
- grad_second_gain: float32 [768], replicated
- grad_second_shift: float32 [768], replicated
- grad_w_query: float32 [768, 768], P('dp', 'tensor')
- grad_w_key: float32 [768, 768], P('dp', 'tensor')
- grad_w_value: float32 [768, 768], P('dp', 'tensor')
- grad_query_bias: float32 [768], P('tensor')
- grad_key_bias: float32 [768], P('tensor')
- grad_value_bias: float32 [768], P('tensor')
- grad_w_out: float32 [768, 768], P('tensor', 'dp')
- grad_out_bias: float32 [768], replicated
- grad_w_up: float32 [768, 3072], P('dp', 'tensor')
- grad_up_bias: float32 [3072], P('tensor')
- grad_w_down: float32 [3072, 768], P('tensor', 'dp')
- grad_down_bias: float32 [768], replicated
The draws below stay inside these ranges and needn't reach their ends.
Inputs may be any that keep to these rules, and one draw needn't show every extreme that they name: Each row of positions holds every position 0 to 4095 exactly once.
All inputs are finite; a program needn't handle non-finite values.
Results may differ from the reference program's by a relative error of at most 0.014.
Values may be sent and summed in bfloat16 or wider, within the bound.
A program may use at most 256 MiB of HBM per device.

```python
import math
import jax
import jax.numpy as jnp
from jax import lax

D = 768
FF = 3072
HEAD_DIM = 64
ROT_DIM = 16
LEN = 4096
SEQUENCES = 4


def block_scale(rng, extent, pieces, low, high):
    loudness = 1.0
    for axis_at, blocks in pieces:
        heights = jax.random.uniform(jax.random.fold_in(jax.random.fold_in(rng, 6), axis_at), (blocks,), jnp.float32, low / len(pieces), high / len(pieces))
        loudness = loudness * jnp.repeat(jnp.exp(heights), extent[axis_at] // blocks).reshape((-1,) + (1,) * (len(extent) - 1 - axis_at))
    return loudness


def normal_values(stream_key, shape, deviation, limit, split=(), kind=jnp.bfloat16):
    array = jax.random.normal(stream_key, shape, jnp.float32) * deviation
    if len(split) > 0:
        array = block_scale(stream_key, shape, split, -0.22, 0.18) * array
    return jnp.clip(array, min=-limit, max=limit).astype(kind)


def setup_inputs(seed: int = 0) -> dict:
    keys = jax.random.split(jax.random.key(seed), 20)
    tokens = normal_values(keys[0], (SEQUENCES, LEN, D), 1.0, 6.0, ((0, 4), (1, 4)))
    positions = jax.vmap(lambda own: jax.random.permutation(own, LEN))(jax.random.split(keys[1], SEQUENCES)).reshape((SEQUENCES, LEN)).astype(jnp.int32)
    first_gain = jnp.clip(1.0 + 0.1 * jax.random.normal(keys[2], (D,), jnp.float32), 0.5, 1.5)
    first_shift = normal_values(keys[3], (D,), 0.3, 3.0, (), jnp.float32)
    second_gain = jnp.clip(1.0 + 0.1 * jax.random.normal(keys[4], (D,), jnp.float32), 0.5, 1.5)
    second_shift = normal_values(keys[5], (D,), 0.3, 3.0, (), jnp.float32)
    w_query = normal_values(keys[6], (D, D), D ** -0.5, 0.21875, ((0, 4), (1, 2)))
    w_key = normal_values(keys[7], (D, D), D ** -0.5, 0.21875, ((0, 4), (1, 2)))
    w_value = normal_values(keys[8], (D, D), D ** -0.5, 0.21875, ((0, 4), (1, 2)))
    query_bias = normal_values(keys[9], (D,), 0.3, 3.0, ((0, 2),), jnp.float32)
    key_bias = normal_values(keys[10], (D,), 0.3, 3.0, ((0, 2),), jnp.float32)
    value_bias = normal_values(keys[11], (D,), 0.3, 3.0, ((0, 2),), jnp.float32)
    w_out = normal_values(keys[12], (D, D), (D // 16) ** -0.5, 0.875, ((0, 2), (1, 4)))
    out_bias = normal_values(keys[13], (D,), 0.3, 3.0, (), jnp.float32)
    w_up = normal_values(keys[14], (D, FF), D ** -0.5, 0.21875, ((0, 4), (1, 2)))
    up_bias = normal_values(keys[15], (FF,), 0.3, 3.0, ((0, 2),), jnp.float32)
    w_down = normal_values(keys[16], (FF, D), FF ** -0.5, 0.109375, ((0, 2), (1, 4)))
    down_bias = normal_values(keys[17], (D,), 0.3, 3.0, (), jnp.float32)
    cotangent = normal_values(keys[18], (SEQUENCES, LEN, D), 1.0, 6.0, ((0, 4), (1, 4)))
    return dict(tokens=tokens, positions=positions, first_gain=first_gain, first_shift=first_shift, second_gain=second_gain, second_shift=second_shift, w_query=w_query, w_key=w_key, w_value=w_value, query_bias=query_bias, key_bias=key_bias, value_bias=value_bias, w_out=w_out, out_bias=out_bias, w_up=w_up, up_bias=up_bias, w_down=w_down, down_bias=down_bias, cotangent=cotangent)


@jax.custom_vjp
def low(v):
    return lax.optimization_barrier(v.astype(jnp.bfloat16)).astype(jnp.float32)

@jax.custom_vjp
def low_back(v):
    return v

def low_keep(v):
    return (low(v), None)

def low_pass(kept, grad):
    return (grad,)

def back_keep(v):
    return (v, None)

def back_low(kept, grad):
    return (low(grad),)
low.defvjp(low_keep, low_pass)
low_back.defvjp(back_keep, back_low)
epsilon = 1e-05

def exact_dot(left, right):
    return jnp.dot(left, right, precision=lax.Precision.HIGHEST)

def layer_norm(values, gain, shift):
    row_mean = lax.optimization_barrier(jnp.mean(values, axis=-1, keepdims=True))
    centred = values - row_mean
    row_var = lax.optimization_barrier(jnp.mean(centred * centred, axis=-1, keepdims=True))
    return centred * lax.rsqrt(row_var + epsilon) * gain + shift

def rotary_tables(places):
    frequency = jnp.exp(jnp.arange(ROT_DIM // 2, dtype=jnp.float32) * (-2.0 * math.log(10000.0) / ROT_DIM))
    angle_rad = places.astype(jnp.float32)[..., None] * frequency
    return (jnp.cos(angle_rad), jnp.sin(angle_rad))

def rotate_heads(field, cosine, sine):
    half_rot = ROT_DIM // 2
    leading = field[..., :half_rot]
    trailing = field[..., half_rot:ROT_DIM]
    return jnp.concatenate([leading * cosine - trailing * sine, trailing * cosine + leading * sine, field[..., ROT_DIM:]], axis=-1)

def head_attend(query_head, key_head, value_head, allowed):
    scores = jnp.dot(query_head, key_head.T, precision=lax.Precision.HIGHEST) * HEAD_DIM ** (-0.5)
    scores = low_back(scores)
    scores = jnp.where(allowed, scores, -1e+30)
    row_max = lax.optimization_barrier(jnp.max(scores, axis=-1, keepdims=True))
    exp_scores = jnp.exp(scores - row_max)
    probs_low = low(exp_scores / lax.optimization_barrier(jnp.sum(exp_scores, axis=-1, keepdims=True)))
    return jnp.dot(probs_low, value_head, precision=lax.Precision.HIGHEST)

def one_sequence(tokens_in, places, params):
    first_gain, first_shift, second_gain, second_shift, w_query, w_key, w_value, query_bias, key_bias, value_bias, w_out, out_bias, w_up, up_bias, w_down, down_bias = params
    seq_len = tokens_in.shape[0]
    head_count = D // HEAD_DIM
    cosine, sine = rotary_tables(places)
    cosine = cosine[:, None, :]
    sine = sine[:, None, :]
    normed_one = low(layer_norm(tokens_in, first_gain, first_shift))
    normed_two = low(layer_norm(tokens_in, second_gain, second_shift))
    query_pre = low_back(exact_dot(normed_one, w_query) + query_bias).reshape(seq_len, head_count, HEAD_DIM)
    key_pre = low_back(exact_dot(normed_one, w_key) + key_bias).reshape(seq_len, head_count, HEAD_DIM)
    value_low = low(low_back(exact_dot(normed_one, w_value) + value_bias)).reshape(seq_len, head_count, HEAD_DIM)
    query_rot = low(rotate_heads(query_pre, cosine, sine))
    key_rot = low(rotate_heads(key_pre, cosine, sine))
    allowed = places[None, :] <= places[:, None]
    head_fn = jax.checkpoint(head_attend)

    def each_head(triple):
        return head_fn(triple[0], triple[1], triple[2], allowed)
    mixed_heads = lax.map(each_head, (query_rot.transpose(1, 0, 2), key_rot.transpose(1, 0, 2), value_low.transpose(1, 0, 2)))
    mixed_out = low(low_back(mixed_heads.transpose(1, 0, 2).reshape(seq_len, D)))
    attended = exact_dot(mixed_out, w_out) + out_bias
    inner_pre = low_back(exact_dot(normed_two, w_up) + up_bias)
    hidden = low(jax.nn.gelu(inner_pre, approximate=False))
    fed_out = exact_dot(hidden, w_down) + down_bias
    return tokens_in + attended + fed_out

def reference(tokens, positions, first_gain, first_shift, second_gain, second_shift, w_query, w_key, w_value, query_bias, key_bias, value_bias, w_out, out_bias, w_up, up_bias, w_down, down_bias, cotangent):
    params = tuple((weight_in.astype(jnp.float32) for weight_in in (first_gain, first_shift, second_gain, second_shift, w_query, w_key, w_value, query_bias, key_bias, value_bias, w_out, out_bias, w_up, up_bias, w_down, down_bias)))
    step_fn = jax.checkpoint(one_sequence)

    def forward(tokens_in, params_in):

        def each_seq(pair_in):
            return step_fn(pair_in[0], pair_in[1], params_in)
        return lax.map(each_seq, (tokens_in, positions))
    block_out, pullback = jax.vjp(forward, tokens.astype(jnp.float32), params)
    grad_tokens, grads = pullback(cotangent.astype(jnp.float32))
    return (block_out.astype(jnp.bfloat16), grad_tokens, grads[0], grads[1], grads[2], grads[3], grads[4], grads[5], grads[6], grads[7], grads[8], grads[9], grads[10], grads[11], grads[12], grads[13], grads[14], grads[15])
```

```python
import math

import jax
import jax.numpy as jnp
from jax import lax
from jax.experimental import pallas as pl
from jax.experimental.pallas import tpu as pltpu
from jax.sharding import PartitionSpec as P

HEAD_DIM = 64
ROT_DIM = 16


epsilon = 1e-05


def rotary_tables(places):
    frequency = jnp.exp(
        jnp.arange(ROT_DIM // 2, dtype=jnp.float32) * (-2.0 * math.log(10000.0) / ROT_DIM)
    )
    angle_rad = places.astype(jnp.float32)[..., None] * frequency
    return (jnp.cos(angle_rad), jnp.sin(angle_rad))


def rotate_rows(field, cosine, sine):
    half_rot = ROT_DIM // 2
    width, row_count = field.shape
    heads = field.reshape(width // HEAD_DIM, HEAD_DIM, row_count)
    leading = heads[:, :half_rot]
    trailing = heads[:, half_rot:ROT_DIM]
    return jnp.concatenate(
        [
            leading * cosine - trailing * sine,
            trailing * cosine + leading * sine,
            heads[:, ROT_DIM:],
        ],
        axis=1,
    ).reshape(width, row_count)


def normalize(values):
    row_mean = jnp.mean(values, axis=-1, keepdims=True)
    centred = values - row_mean
    row_var = jnp.mean(centred * centred, axis=-1, keepdims=True)
    inv_std = lax.rsqrt(row_var + epsilon)
    return (centred * inv_std, inv_std)


def fold_rows(field, how):
    rows, lanes = field.shape
    return how(field.reshape(rows // 8, 8, lanes), axis=0)


def attend_kernel(
    query_places,
    key_places,
    query_ref,
    key_ref,
    value_ref,
    grad_ref,
    mixed_ref,
    grad_query_ref,
    grad_key_ref,
    grad_value_ref,
    key_rows,
    value_rows,
    key_sum,
    value_sum,
    score_buf,
    prob_buf,
):
    chunks, chunk_len, query_len = score_buf.shape
    block = pl.program_id(2)

    @pl.when(block == 0)
    def _():
        def turn(c, carry):
            key_rows[c] = key_ref[c].T
            value_rows[c] = value_ref[c].T
            key_sum[c] = jnp.zeros_like(key_sum[c])
            value_sum[c] = jnp.zeros_like(value_sum[c])
            return carry

        lax.fori_loop(0, chunks, turn, 0)

    scale = HEAD_DIM ** (-0.5)
    query = query_ref[...]
    grad = grad_ref[...]
    query_scaled = query * jnp.bfloat16(scale)
    own_places = query_places[0]

    def score_step(c, top):
        scores = jnp.dot(key_rows[c], query_scaled, preferred_element_type=jnp.float32)
        places = jnp.concatenate([key_places[c]] * (query_len // 128), axis=1)
        scores = jnp.where(places <= own_places, scores, -1e30)
        score_buf[c] = scores
        return jnp.maximum(top, fold_rows(scores, jnp.max))

    top = lax.fori_loop(
        0, chunks, score_step, jnp.full((8, query_len), -1e30, jnp.float32)
    )
    row_max = jnp.max(top, axis=0, keepdims=True)

    def prob_step(c, carry):
        total, mixed = carry
        probs = jnp.exp(score_buf[c] - row_max)
        low = probs.astype(jnp.bfloat16)
        prob_buf[c] = low
        mixed = mixed + jnp.dot(value_ref[c], low, preferred_element_type=jnp.float32)
        return total + fold_rows(probs, jnp.sum), mixed

    total, mixed = lax.fori_loop(
        0,
        chunks,
        prob_step,
        (
            jnp.zeros((8, query_len), jnp.float32),
            jnp.zeros((HEAD_DIM, query_len), jnp.float32),
        ),
    )
    inverse = 1.0 / jnp.sum(total, axis=0, keepdims=True)
    mixed = mixed * inverse
    mixed_ref[...] = mixed.astype(jnp.bfloat16)
    delta = jnp.sum(mixed * grad.astype(jnp.float32), axis=0, keepdims=True)
    query_back = (query.astype(jnp.float32) * (inverse * scale)).T.astype(jnp.bfloat16)
    grad_back = (grad.astype(jnp.float32) * inverse).T.astype(jnp.bfloat16)

    def back_step(c, grad_query):
        low = prob_buf[c]
        grad_probs = jnp.dot(value_rows[c], grad, preferred_element_type=jnp.float32)
        grad_scores = (low.astype(jnp.float32) * (grad_probs - delta)).astype(jnp.bfloat16)
        value_sum[c] += jnp.dot(low, grad_back, preferred_element_type=jnp.float32)
        key_sum[c] += jnp.dot(grad_scores, query_back, preferred_element_type=jnp.float32)
        return grad_query + jnp.dot(
            key_ref[c], grad_scores, preferred_element_type=jnp.float32
        )

    grad_query = lax.fori_loop(
        0, chunks, back_step, jnp.zeros((HEAD_DIM, query_len), jnp.float32)
    )
    grad_query_ref[...] = grad_query * (inverse * scale)

    @pl.when(block == pl.num_programs(2) - 1)
    def _():
        def turn(c, carry):
            grad_key_ref[c] = key_sum[c].T.astype(jnp.bfloat16)
            grad_value_ref[c] = value_sum[c].T.astype(jnp.bfloat16)
            return carry

        lax.fori_loop(0, chunks, turn, 0)


def attend(query, key_value, grad, own_places, all_places, seq_count, block_len):
    width, row_count = query.shape
    chunks = key_value.shape[0]
    heads = width // HEAD_DIM
    query_len = 512 if block_len % 512 == 0 else block_len
    blocks = block_len // query_len
    column_places = jnp.broadcast_to(
        all_places.reshape(chunks, row_count)[..., None], (chunks, row_count, 128)
    )
    row_places = own_places.reshape(row_count // query_len, 1, query_len)
    one = pl.BlockSpec((HEAD_DIM, query_len), lambda s, h, i: (h, s * blocks + i))
    every = pl.BlockSpec((chunks, HEAD_DIM, block_len), lambda s, h, i: (0, h, s))
    pairs = row_count * chunks * block_len * heads
    return pl.pallas_call(
        attend_kernel,
        grid=(seq_count, heads, blocks),
        in_specs=[
            pl.BlockSpec((1, 1, query_len), lambda s, h, i: (s * blocks + i, 0, 0)),
            pl.BlockSpec((chunks, block_len, 128), lambda s, h, i: (0, s, 0)),
            one,
            every,
            pl.BlockSpec((chunks, HEAD_DIM, block_len), lambda s, h, i: (0, h + heads, s)),
            one,
        ],
        out_specs=[one, one, every, every],
        out_shape=[
            jax.ShapeDtypeStruct((width, row_count), jnp.bfloat16),
            jax.ShapeDtypeStruct((width, row_count), jnp.float32),
            jax.ShapeDtypeStruct((chunks, width, row_count), jnp.bfloat16),
            jax.ShapeDtypeStruct((chunks, width, row_count), jnp.bfloat16),
        ],
        scratch_shapes=[
            pltpu.VMEM((chunks, block_len, HEAD_DIM), jnp.bfloat16),
            pltpu.VMEM((chunks, block_len, HEAD_DIM), jnp.bfloat16),
            pltpu.VMEM((chunks, block_len, HEAD_DIM), jnp.float32),
            pltpu.VMEM((chunks, block_len, HEAD_DIM), jnp.float32),
            pltpu.VMEM((chunks, block_len, query_len), jnp.float32),
            pltpu.VMEM((chunks, block_len, query_len), jnp.bfloat16),
        ],
        compiler_params=pltpu.CompilerParams(vmem_limit_bytes=50 * 2**20),
        cost_estimate=pl.CostEstimate(
            flops=48 * pairs * HEAD_DIM, bytes_accessed=32 * 2**20, transcendentals=pairs
        ),
    )(row_places, column_places, query, key_value, key_value, grad)


def over_tensor(part):
    low = part.astype(jnp.bfloat16)
    count = lax.axis_size("tensor")
    if count != 2:
        return lax.psum(low, "tensor").astype(jnp.float32)
    other = lax.ppermute(low, "tensor", [(0, 1), (1, 0)])
    return low.astype(jnp.float32) + other.astype(jnp.float32)


def owner_sum(grads):
    own = lax.psum_scatter(grads.astype(jnp.bfloat16), "dp", scatter_dimension=0, tiled=True)
    return lax.psum(own, "context").astype(jnp.float32)


def body(
    tokens,
    positions,
    first_gain,
    first_shift,
    second_gain,
    second_shift,
    w_query,
    w_key,
    w_value,
    query_bias,
    key_bias,
    value_bias,
    w_out,
    out_bias,
    w_up,
    up_bias,
    w_down,
    down_bias,
    cotangent,
):
    seq_count, block_len, model_width = tokens.shape
    row_count = seq_count * block_len
    flat_in = tokens.reshape(row_count, model_width).astype(jnp.float32)
    upstream = cotangent.reshape(row_count, model_width)
    ff_part = w_up.shape[1]
    part_width = w_query.shape[1]
    half_rot = ROT_DIM // 2
    f32 = jnp.float32
    low = jnp.bfloat16

    def mm(spec, left, right):
        return jnp.einsum(spec, left, right, preferred_element_type=f32)

    full_qkv = lax.all_gather(
        jnp.concatenate([w_query, w_key, w_value], axis=1), "dp", axis=0, tiled=True
    )
    places = lax.all_gather(positions, "context", axis=0, tiled=False)
    full_rest = lax.all_gather(
        jnp.concatenate([w_up, w_down.T, w_out.T], axis=1), "dp", axis=0, tiled=True
    )
    full_up = full_rest[:, :ff_part]
    full_down = full_rest[:, ff_part : 2 * ff_part]
    full_out = full_rest[:, 2 * ff_part :]

    plain, inv_std = normalize(flat_in)
    normed_one = (plain * first_gain + first_shift).astype(low)
    normed_two = (plain * second_gain + second_shift).astype(low)
    cosine, sine = rotary_tables(positions)
    cosine = cosine.reshape(row_count, half_rot).T
    sine = sine.reshape(row_count, half_rot).T

    qkv_bias = jnp.concatenate([query_bias, key_bias, value_bias])
    qkv = mm("dc,rd->cr", full_qkv, normed_one) + qkv_bias[:, None]
    query = rotate_rows(qkv[:part_width], cosine, sine).astype(low)
    key = rotate_rows(qkv[part_width : 2 * part_width], cosine, sine).astype(low)
    value = qkv[2 * part_width :].astype(low)
    key_value = lax.all_gather(
        jnp.concatenate([key, value], axis=0), "context", axis=0, tiled=False
    )

    grad_mixed = mm("dc,rd->cr", full_out, upstream).astype(low)
    inner = mm("rd,df->rf", normed_two, full_up) + up_bias
    below = 0.5 * (1.0 + lax.erf(inner * (0.5**0.5)))
    hidden = (inner * below).astype(low)
    slope = below + inner * jnp.exp(-0.5 * inner * inner) * ((2.0 * math.pi) ** -0.5)
    grad_inner = (mm("rd,df->rf", upstream, full_down) * slope).astype(low)
    grad_ff = jnp.concatenate(
        [mm("rd,rf->df", normed_two, grad_inner), mm("rd,rf->df", upstream, hidden)], axis=1
    )
    own_ff = owner_sum(grad_ff)
    back_two = mm("rf,df->rd", grad_inner, full_up)
    out_two = mm("rf,df->rd", hidden, full_down)
    upstream_wide = upstream.astype(f32)

    mixed, grad_query_rot, grad_key_all, grad_value_all = attend(
        query, key_value, grad_mixed, positions, places, seq_count, block_len
    )
    key_part = lax.psum_scatter(grad_key_all, "context", scatter_dimension=0, tiled=False)
    value_part = lax.psum_scatter(grad_value_all, "context", scatter_dimension=0, tiled=False)

    summed = over_tensor(mm("cr,dc->rd", mixed, full_out) + out_two)
    block_out = (
        (flat_in + summed + out_bias + down_bias)
        .astype(low)
        .reshape(seq_count, block_len, model_width)
    )

    grad_qkv = jnp.concatenate(
        [
            rotate_rows(grad_query_rot, cosine, -sine).astype(low),
            rotate_rows(key_part.astype(f32), cosine, -sine).astype(low),
            value_part,
        ],
        axis=0,
    )
    back_one = mm("cr,dc->rd", grad_qkv, full_qkv)
    tilted = over_tensor(back_one * first_gain + back_two * second_gain)
    first_mean = jnp.mean(tilted, axis=-1, keepdims=True)
    second_mean = jnp.mean(tilted * plain, axis=-1, keepdims=True)
    grad_tokens = (
        upstream_wide + inv_std * (tilted - first_mean - plain * second_mean)
    ).reshape(seq_count, block_len, model_width)

    grad_late = jnp.concatenate(
        [mm("rd,cr->dc", upstream, mixed), mm("rd,cr->dc", normed_one, grad_qkv)], axis=1
    )
    own_late = owner_sum(grad_late)

    gains = jnp.stack(
        [
            jnp.sum(back_one * plain, axis=0),
            jnp.sum(back_one, axis=0),
            jnp.sum(back_two * plain, axis=0),
            jnp.sum(back_two, axis=0),
        ]
    ).reshape(-1)
    biases = jnp.concatenate(
        [
            jnp.sum(grad_qkv.astype(f32), axis=1),
            jnp.sum(grad_inner.astype(f32), axis=0),
            jnp.sum(upstream_wide, axis=0),
        ]
    )
    vectors = lax.all_gather(
        jnp.concatenate([gains, biases]), ("tensor", "dp", "context"), axis=0, tiled=False
    )
    sum_g1, sum_s1, sum_g2, sum_s2 = jnp.sum(vectors[:, : gains.shape[0]], axis=0).reshape(
        4, model_width
    )
    sides = lax.axis_size("tensor")
    own_side = lax.dynamic_index_in_dim(
        vectors[:, gains.shape[0] :].reshape(sides, -1, biases.shape[0]),
        lax.axis_index("tensor"),
        0,
        keepdims=False,
    )
    sum_b = jnp.sum(own_side, axis=0)
    cuts = [part_width, 2 * part_width, 3 * part_width, 3 * part_width + ff_part]
    sum_qb, sum_kb, sum_vb, sum_ub, sum_ob = jnp.split(sum_b, cuts)
    shard_out, shard_query, shard_key, shard_value = jnp.split(own_late, 4, axis=1)
    shard_up = own_ff[:, :ff_part]
    shard_down = own_ff[:, ff_part:].T
    shard_out = shard_out.T
    return (
        block_out,
        grad_tokens,
        sum_g1,
        sum_s1,
        sum_g2,
        sum_s2,
        shard_query,
        shard_key,
        shard_value,
        sum_qb,
        sum_kb,
        sum_vb,
        shard_out,
        sum_ob,
        shard_up,
        sum_ub,
        shard_down,
        sum_ob,
    )


def solution(mesh):
    return jax.shard_map(
        body,
        mesh=mesh,
        in_specs=(
            P("dp", "context", None),
            P("dp", "context"),
            P(),
            P(),
            P(),
            P(),
            P("dp", "tensor"),
            P("dp", "tensor"),
            P("dp", "tensor"),
            P("tensor"),
            P("tensor"),
            P("tensor"),
            P("tensor", "dp"),
            P(),
            P("dp", "tensor"),
            P("tensor"),
            P("tensor", "dp"),
            P(),
            P("dp", "context", None),
        ),
        out_specs=(
            P("dp", "context", None),
            P("dp", "context", None),
            P(),
            P(),
            P(),
            P(),
            P("dp", "tensor"),
            P("dp", "tensor"),
            P("dp", "tensor"),
            P("tensor"),
            P("tensor"),
            P("tensor"),
            P("tensor", "dp"),
            P(),
            P("dp", "tensor"),
            P("tensor"),
            P("tensor", "dp"),
            P(),
        ),
        check_vma=False,
    )
```

```python
import math

import jax
import jax.numpy as jnp
from jax import lax
from jax.experimental import pallas as pl
from jax.experimental.pallas import tpu as pltpu
from jax.sharding import PartitionSpec as P

HEAD_DIM = 64
ROT_DIM = 16


epsilon = 1e-05


def rotary_tables(places):
    frequency = jnp.exp(
        jnp.arange(ROT_DIM // 2, dtype=jnp.float32) * (-2.0 * math.log(10000.0) / ROT_DIM)
    )
    angle_rad = places.astype(jnp.float32)[..., None] * frequency
    return (jnp.cos(angle_rad), jnp.sin(angle_rad))


def rotate_rows(field, cosine, sine):
    half_rot = ROT_DIM // 2
    width, row_count = field.shape
    heads = field.reshape(width // HEAD_DIM, HEAD_DIM, row_count)
    leading = heads[:, :half_rot]
    trailing = heads[:, half_rot:ROT_DIM]
    return jnp.concatenate(
        [
            leading * cosine - trailing * sine,
            trailing * cosine + leading * sine,
            heads[:, ROT_DIM:],
        ],
        axis=1,
    ).reshape(width, row_count)


def normalize(values):
    row_mean = jnp.mean(values, axis=-1, keepdims=True)
    centred = values - row_mean
    row_var = jnp.mean(centred * centred, axis=-1, keepdims=True)
    inv_std = lax.rsqrt(row_var + epsilon)
    return (centred * inv_std, inv_std)


def fold_rows(field, how):
    rows, lanes = field.shape
    return how(field.reshape(rows // 8, 8, lanes), axis=0)


def attend_kernel(
    query_places,
    key_places,
    query_ref,
    key_ref,
    value_ref,
    grad_ref,
    mixed_ref,
    grad_query_ref,
    grad_pair_ref,
    key_rows,
    value_rows,
    key_sum,
    value_sum,
    score_buf,
):
    chunks, chunk_len, query_len = score_buf.shape
    block = pl.program_id(2)

    @pl.when(block == 0)
    def _():
        def turn(c, carry):
            key_rows[c] = key_ref[c].T
            value_rows[c] = value_ref[c].T
            key_sum[c] = jnp.zeros_like(key_sum[c])
            value_sum[c] = jnp.zeros_like(value_sum[c])
            return carry

        lax.fori_loop(0, chunks, turn, 0)

    scale = HEAD_DIM ** (-0.5)
    query = query_ref[...]
    grad = grad_ref[...]
    query_scaled = query * jnp.bfloat16(scale)
    own_places = query_places[0]

    def score_step(c, top):
        scores = jnp.dot(key_rows[c], query_scaled, preferred_element_type=jnp.float32)
        places = jnp.concatenate([key_places[c]] * (query_len // 128), axis=1)
        scores = jnp.where(places <= own_places, scores, -1e30)
        score_buf[c] = scores
        return jnp.maximum(top, fold_rows(scores, jnp.max))

    top = lax.fori_loop(
        0, chunks, score_step, jnp.full((8, query_len), -1e30, jnp.float32)
    )
    row_max = jnp.max(top, axis=0, keepdims=True)

    def prob_step(c, carry):
        total, mixed = carry
        probs = jnp.exp(score_buf[c] - row_max)
        low = probs.astype(jnp.bfloat16)
        score_buf[c] = probs
        mixed = mixed + jnp.dot(value_ref[c], low, preferred_element_type=jnp.float32)
        return total + fold_rows(probs, jnp.sum), mixed

    total, mixed = lax.fori_loop(
        0,
        chunks,
        prob_step,
        (
            jnp.zeros((8, query_len), jnp.float32),
            jnp.zeros((HEAD_DIM, query_len), jnp.float32),
        ),
    )
    inverse = 1.0 / jnp.sum(total, axis=0, keepdims=True)
    mixed = mixed * inverse
    mixed_ref[...] = mixed.astype(jnp.bfloat16)
    delta = jnp.sum(mixed * grad.astype(jnp.float32), axis=0, keepdims=True)
    query_back = (query.astype(jnp.float32) * (inverse * scale)).T.astype(jnp.bfloat16)
    grad_back = (grad.astype(jnp.float32) * inverse).T.astype(jnp.bfloat16)

    def back_step(c, grad_query):
        probs = score_buf[c]
        low = probs.astype(jnp.bfloat16)
        grad_probs = jnp.dot(value_rows[c], grad, preferred_element_type=jnp.float32)
        grad_scores = (probs * (grad_probs - delta)).astype(jnp.bfloat16)
        value_sum[c] += jnp.dot(low, grad_back, preferred_element_type=jnp.float32)
        key_sum[c] += jnp.dot(grad_scores, query_back, preferred_element_type=jnp.float32)
        return grad_query + jnp.dot(
            key_ref[c], grad_scores, preferred_element_type=jnp.float32
        )

    grad_query = lax.fori_loop(
        0, chunks, back_step, jnp.zeros((HEAD_DIM, query_len), jnp.float32)
    )
    grad_query_ref[...] = grad_query * (inverse * scale)

    @pl.when(block == pl.num_programs(2) - 1)
    def _():
        def turn(c, carry):
            grad_pair_ref[c, 0] = key_sum[c].T.astype(jnp.bfloat16)
            grad_pair_ref[c, 1] = value_sum[c].T.astype(jnp.bfloat16)
            return carry

        lax.fori_loop(0, chunks, turn, 0)


def attend(query, key_value, grad, own_places, all_places, seq_count, block_len):
    width, row_count = query.shape
    chunks = key_value.shape[0]
    heads = width // HEAD_DIM
    query_len = 512 if block_len % 512 == 0 else block_len
    blocks = block_len // query_len
    column_places = jnp.broadcast_to(
        all_places.reshape(chunks, row_count)[..., None], (chunks, row_count, 128)
    )
    row_places = own_places.reshape(row_count // query_len, 1, query_len)
    one = pl.BlockSpec((HEAD_DIM, query_len), lambda s, h, i: (h, s * blocks + i))
    every = pl.BlockSpec((chunks, HEAD_DIM, block_len), lambda s, h, i: (0, h, s))
    pairs = row_count * chunks * block_len * heads
    return pl.pallas_call(
        attend_kernel,
        grid=(seq_count, heads, blocks),
        in_specs=[
            pl.BlockSpec((1, 1, query_len), lambda s, h, i: (s * blocks + i, 0, 0)),
            pl.BlockSpec((chunks, block_len, 128), lambda s, h, i: (0, s, 0)),
            one,
            every,
            pl.BlockSpec((chunks, HEAD_DIM, block_len), lambda s, h, i: (0, h + heads, s)),
            one,
        ],
        out_specs=[
            one,
            one,
            pl.BlockSpec((chunks, 2, HEAD_DIM, block_len), lambda s, h, i: (0, 0, h, s)),
        ],
        out_shape=[
            jax.ShapeDtypeStruct((width, row_count), jnp.bfloat16),
            jax.ShapeDtypeStruct((width, row_count), jnp.float32),
            jax.ShapeDtypeStruct((chunks, 2, width, row_count), jnp.bfloat16),
        ],
        scratch_shapes=[
            pltpu.VMEM((chunks, block_len, HEAD_DIM), jnp.bfloat16),
            pltpu.VMEM((chunks, block_len, HEAD_DIM), jnp.bfloat16),
            pltpu.VMEM((chunks, block_len, HEAD_DIM), jnp.float32),
            pltpu.VMEM((chunks, block_len, HEAD_DIM), jnp.float32),
            pltpu.VMEM((chunks, block_len, query_len), jnp.float32),
        ],
        compiler_params=pltpu.CompilerParams(vmem_limit_bytes=50 * 2**20),
        cost_estimate=pl.CostEstimate(
            flops=48 * pairs * HEAD_DIM, bytes_accessed=32 * 2**20, transcendentals=pairs
        ),
    )(row_places, column_places, query, key_value, key_value, grad)


def over_tensor(part):
    low = part.astype(jnp.bfloat16)
    count = lax.axis_size("tensor")
    if count != 2:
        return lax.psum(low, "tensor").astype(jnp.float32)
    other = lax.ppermute(low, "tensor", [(0, 1), (1, 0)])
    return low.astype(jnp.float32) + other.astype(jnp.float32)


def gather_rows(shard):
    count = lax.axis_size("dp")
    chips = count // 2
    here = lax.axis_index("dp")
    parts = [shard] + [
        lax.ppermute(shard, "dp", [(i, (i + 2 * step) % count) for i in range(count)])
        for step in range(1, chips)
    ]
    parts = jnp.stack(parts)
    other = lax.ppermute(parts, "dp", [(i, i ^ 1) for i in range(count)])
    first = here % 2 == 0
    even = jnp.where(first, parts, other)
    odd = jnp.where(first, other, parts)
    both = jnp.stack([even, odd], axis=1)
    ordered = [
        lax.dynamic_index_in_dim(both, (here // 2 - chip) % chips, 0, keepdims=False)
        for chip in range(chips)
    ]
    return jnp.stack(ordered).reshape(count * shard.shape[0], shard.shape[1])


def scatter_core(grads):
    count = lax.axis_size("dp")
    core = lax.axis_index("dp") % 2
    split = grads.astype(jnp.bfloat16).reshape(count // 2, 2, -1, grads.shape[1])
    keep = lax.dynamic_index_in_dim(split, core, 1, keepdims=False)
    send = lax.dynamic_index_in_dim(split, 1 - core, 1, keepdims=False)
    other = lax.ppermute(send, "dp", [(i, i ^ 1) for i in range(count)])
    return (keep.astype(jnp.float32) + other.astype(jnp.float32)).astype(jnp.bfloat16)


def scatter_chips(half):
    count = lax.axis_size("dp")
    chips = count // 2
    chip = lax.axis_index("dp") // 2
    total = lax.dynamic_index_in_dim(half, chip, 0, keepdims=False).astype(jnp.float32)
    for step in range(1, chips):
        send = lax.dynamic_index_in_dim(half, (chip + step) % chips, 0, keepdims=False)
        other = lax.ppermute(
            send, "dp", [(i, (i + 2 * step) % count) for i in range(count)]
        )
        total = total + other.astype(jnp.float32)
    return total.astype(jnp.bfloat16)


def small_sum(vector, axis):
    count = lax.axis_size(axis)
    here = lax.axis_index(axis)
    parts = [vector] + [
        lax.ppermute(vector, axis, [(i, (i + step) % count) for i in range(count)])
        for step in range(1, count)
    ]
    parts = jnp.stack(parts)
    total = lax.dynamic_index_in_dim(parts, here % count, 0, keepdims=False)
    for owner in range(1, count):
        total = total + lax.dynamic_index_in_dim(
            parts, (here - owner) % count, 0, keepdims=False
        )
    return total


def body(
    tokens,
    positions,
    first_gain,
    first_shift,
    second_gain,
    second_shift,
    w_query,
    w_key,
    w_value,
    query_bias,
    key_bias,
    value_bias,
    w_out,
    out_bias,
    w_up,
    up_bias,
    w_down,
    down_bias,
    cotangent,
):
    seq_count, block_len, model_width = tokens.shape
    row_count = seq_count * block_len
    flat_in = tokens.reshape(row_count, model_width).astype(jnp.float32)
    upstream = cotangent.reshape(row_count, model_width)
    ff_part = w_up.shape[1]
    part_width = w_query.shape[1]
    half_rot = ROT_DIM // 2
    f32 = jnp.float32
    low = jnp.bfloat16

    def mm(spec, left, right):
        return jnp.einsum(spec, left, right, preferred_element_type=f32)

    groups = 2 if (part_width // HEAD_DIM) % 2 == 0 else 1
    group_width = part_width // groups

    places = lax.all_gather(positions, "context", axis=0, tiled=False)
    full_first = gather_rows(jnp.concatenate([w_query, w_key, w_value, w_out.T], axis=1))
    rest = jnp.concatenate([w_up, w_down.T], axis=1)
    full_first, places, rest = lax.optimization_barrier((full_first, places, rest))
    full_qkv = full_first[:, : 3 * part_width]
    full_out = full_first[:, 3 * part_width :]
    full_rest = gather_rows(rest)
    full_up = full_rest[:, :ff_part]
    full_down = full_rest[:, ff_part:]

    plain, inv_std = normalize(flat_in)
    normed_one = (plain * first_gain + first_shift).astype(low)
    normed_two = (plain * second_gain + second_shift).astype(low)
    cosine, sine = rotary_tables(positions)
    cosine = cosine.reshape(row_count, half_rot).T
    sine = sine.reshape(row_count, half_rot).T

    qkv_bias = jnp.concatenate([query_bias, key_bias, value_bias])
    qkv = mm("dc,rd->cr", full_qkv, normed_one) + qkv_bias[:, None]
    query = rotate_rows(qkv[:part_width], cosine, sine).astype(low)
    key = rotate_rows(qkv[part_width : 2 * part_width], cosine, sine).astype(low)
    value = qkv[2 * part_width :].astype(low)
    spans = [slice(g * group_width, (g + 1) * group_width) for g in range(groups)]
    key_values = []
    for span in spans:
        pair = jnp.concatenate([key[span], value[span]], axis=0)
        if key_values:
            pair, key_values[-1] = lax.optimization_barrier((pair, key_values[-1]))
        key_values.append(lax.all_gather(pair, "context", axis=0, tiled=False))

    grad_mixed = mm("dc,rd->cr", full_out, upstream).astype(low)
    inner = mm("rd,df->rf", normed_two, full_up) + up_bias
    below = 0.5 * (1.0 + lax.erf(inner * (0.5**0.5)))
    hidden = (inner * below).astype(low)
    slope = below + inner * jnp.exp(-0.5 * inner * inner) * ((2.0 * math.pi) ** -0.5)
    grad_inner = (mm("rd,df->rf", upstream, full_down) * slope).astype(low)
    grad_ff = jnp.concatenate(
        [mm("rd,rf->df", normed_two, grad_inner), mm("rd,rf->df", upstream, hidden)], axis=1
    )
    half_ff = scatter_core(grad_ff)
    back_two = mm("rf,df->rd", grad_inner, full_up)
    out_two = mm("rf,df->rd", hidden, full_down)
    upstream_wide = upstream.astype(f32)

    query, grad_mixed, half_ff, back_two, out_two = lax.optimization_barrier(
        (query, grad_mixed, half_ff, back_two, out_two)
    )
    quarter_ff = scatter_chips(half_ff)
    mixed, grad_query_rot, key_parts, value_parts = [], [], [], []
    for span, key_value in zip(spans, key_values):
        mixed_part, query_part, pair_all = attend(
            query[span], key_value, grad_mixed[span], positions, places, seq_count, block_len
        )
        pair = lax.psum_scatter(pair_all, "context", scatter_dimension=0, tiled=False)
        mixed.append(mixed_part)
        grad_query_rot.append(query_part)
        key_parts.append(pair[0])
        value_parts.append(pair[1])
    mixed = jnp.concatenate(mixed, axis=0)
    grad_query_rot = jnp.concatenate(grad_query_rot, axis=0)
    summed = over_tensor(mm("cr,dc->rd", mixed, full_out) + out_two)
    grad_out = mm("rd,cr->dc", upstream, mixed)
    quarter_ff, summed, grad_out, value_parts[-1], key_parts[-1] = lax.optimization_barrier(
        (quarter_ff, summed, grad_out, value_parts[-1], key_parts[-1])
    )
    key_part = jnp.concatenate(key_parts, axis=0)
    value_part = jnp.concatenate(value_parts, axis=0)
    own_ff = lax.psum(quarter_ff, "context")
    block_out = (
        (flat_in + summed + out_bias + down_bias)
        .astype(low)
        .reshape(seq_count, block_len, model_width)
    )

    grad_qkv = jnp.concatenate(
        [
            rotate_rows(grad_query_rot, cosine, -sine).astype(low),
            rotate_rows(key_part.astype(f32), cosine, -sine).astype(low),
            value_part,
        ],
        axis=0,
    )
    back_one = mm("cr,dc->rd", grad_qkv, full_qkv)
    tilted = over_tensor(back_one * first_gain + back_two * second_gain)
    first_mean = jnp.mean(tilted, axis=-1, keepdims=True)
    second_mean = jnp.mean(tilted * plain, axis=-1, keepdims=True)
    grad_tokens = (
        upstream_wide + inv_std * (tilted - first_mean - plain * second_mean)
    ).reshape(seq_count, block_len, model_width)

    grad_late = jnp.concatenate(
        [grad_out, mm("rd,cr->dc", normed_one, grad_qkv)], axis=1
    )
    quarter_late, own_ff = lax.optimization_barrier(
        (scatter_chips(scatter_core(grad_late)), own_ff)
    )
    own_late = lax.psum(quarter_late, "context").astype(f32)
    own_ff = own_ff.astype(f32)

    gains = jnp.stack(
        [
            jnp.sum(back_one * plain, axis=0),
            jnp.sum(back_one, axis=0),
            jnp.sum(back_two * plain, axis=0),
            jnp.sum(back_two, axis=0),
        ]
    ).reshape(-1)
    biases = jnp.concatenate(
        [
            jnp.sum(grad_qkv.astype(f32), axis=1),
            jnp.sum(grad_inner.astype(f32), axis=0),
            jnp.sum(upstream_wide, axis=0),
        ]
    )
    vector = jnp.concatenate([gains, biases]).reshape(1, -1)
    vector = small_sum(small_sum(vector, "dp"), "context")
    sum_g = small_sum(vector[:, : gains.shape[0]], "tensor").reshape(4, model_width)
    sum_g1, sum_s1, sum_g2, sum_s2 = sum_g
    sum_b = vector[0, gains.shape[0] :]
    cuts = [part_width, 2 * part_width, 3 * part_width, 3 * part_width + ff_part]
    sum_qb, sum_kb, sum_vb, sum_ub, sum_ob = jnp.split(sum_b, cuts)
    shard_out, shard_query, shard_key, shard_value = jnp.split(own_late, 4, axis=1)
    shard_up = own_ff[:, :ff_part]
    shard_down = own_ff[:, ff_part:].T
    shard_out = shard_out.T
    return (
        block_out,
        grad_tokens,
        sum_g1,
        sum_s1,
        sum_g2,
        sum_s2,
        shard_query,
        shard_key,
        shard_value,
        sum_qb,
        sum_kb,
        sum_vb,
        shard_out,
        sum_ob,
        shard_up,
        sum_ub,
        shard_down,
        sum_ob,
    )


def solution(mesh):
    return jax.shard_map(
        body,
        mesh=mesh,
        in_specs=(
            P("dp", "context", None),
            P("dp", "context"),
            P(),
            P(),
            P(),
            P(),
            P("dp", "tensor"),
            P("dp", "tensor"),
            P("dp", "tensor"),
            P("tensor"),
            P("tensor"),
            P("tensor"),
            P("tensor", "dp"),
            P(),
            P("dp", "tensor"),
            P("tensor"),
            P("tensor", "dp"),
            P(),
            P("dp", "context", None),
        ),
        out_specs=(
            P("dp", "context", None),
            P("dp", "context", None),
            P(),
            P(),
            P(),
            P(),
            P("dp", "tensor"),
            P("dp", "tensor"),
            P("dp", "tensor"),
            P("tensor"),
            P("tensor"),
            P("tensor"),
            P("tensor", "dp"),
            P(),
            P("dp", "tensor"),
            P("tensor"),
            P("tensor", "dp"),
            P(),
        ),
        check_vma=False,
    )
```

```python
import math

import jax
import jax.numpy as jnp
from jax import lax
from jax.experimental import pallas as pl
from jax.experimental.pallas import tpu as pltpu
from jax.sharding import PartitionSpec as P

HEAD_DIM = 64
ROT_DIM = 16


epsilon = 1e-05


def rotary_tables(places):
    frequency = jnp.exp(
        jnp.arange(ROT_DIM // 2, dtype=jnp.float32) * (-2.0 * math.log(10000.0) / ROT_DIM)
    )
    angle_rad = places.astype(jnp.float32)[..., None] * frequency
    return (jnp.cos(angle_rad), jnp.sin(angle_rad))


def rotate_rows(field, cosine, sine):
    half_rot = ROT_DIM // 2
    width, row_count = field.shape
    heads = field.reshape(width // HEAD_DIM, HEAD_DIM, row_count)
    leading = heads[:, :half_rot]
    trailing = heads[:, half_rot:ROT_DIM]
    return jnp.concatenate(
        [
            leading * cosine - trailing * sine,
            trailing * cosine + leading * sine,
            heads[:, ROT_DIM:],
        ],
        axis=1,
    ).reshape(width, row_count)


def normalize(values):
    row_mean = jnp.mean(values, axis=-1, keepdims=True)
    centred = values - row_mean
    row_var = jnp.mean(centred * centred, axis=-1, keepdims=True)
    inv_std = lax.rsqrt(row_var + epsilon)
    return (centred * inv_std, inv_std)


def fold_rows(field, how):
    rows, lanes = field.shape
    return how(field.reshape(rows // 8, 8, lanes), axis=0)


def attend_kernel(
    query_places,
    key_places,
    query_ref,
    key_ref,
    value_ref,
    grad_ref,
    mixed_ref,
    grad_query_ref,
    grad_pair_ref,
    key_rows,
    value_rows,
    key_sum,
    value_sum,
    score_buf,
):
    chunks, chunk_len, query_len = score_buf.shape
    block = pl.program_id(2)

    @pl.when(block == 0)
    def _():
        def turn(c, carry):
            key_rows[c] = key_ref[c].T
            value_rows[c] = value_ref[c].T
            key_sum[c] = jnp.zeros_like(key_sum[c])
            value_sum[c] = jnp.zeros_like(value_sum[c])
            return carry

        lax.fori_loop(0, chunks, turn, 0)

    scale = HEAD_DIM ** (-0.5)
    query = query_ref[...]
    grad = grad_ref[...]
    query_scaled = query * jnp.bfloat16(scale)
    own_places = query_places[0]

    def score_step(c, top):
        scores = jnp.dot(key_rows[c], query_scaled, preferred_element_type=jnp.float32)
        places = jnp.concatenate([key_places[c]] * (query_len // 128), axis=1)
        scores = jnp.where(places <= own_places, scores, -1e30)
        score_buf[c] = scores
        return jnp.maximum(top, fold_rows(scores, jnp.max))

    top = lax.fori_loop(
        0, chunks, score_step, jnp.full((8, query_len), -1e30, jnp.float32)
    )
    row_max = jnp.max(top, axis=0, keepdims=True)

    def prob_step(c, carry):
        total, mixed = carry
        probs = jnp.exp(score_buf[c] - row_max)
        low = probs.astype(jnp.bfloat16)
        probs = low.astype(jnp.float32)
        score_buf[c] = probs
        mixed = mixed + jnp.dot(value_ref[c], low, preferred_element_type=jnp.float32)
        return total + fold_rows(probs, jnp.sum), mixed

    total, mixed = lax.fori_loop(
        0,
        chunks,
        prob_step,
        (
            jnp.zeros((8, query_len), jnp.float32),
            jnp.zeros((HEAD_DIM, query_len), jnp.float32),
        ),
    )
    inverse = 1.0 / jnp.sum(total, axis=0, keepdims=True)
    mixed = mixed * inverse
    mixed_ref[...] = mixed.astype(jnp.bfloat16)
    delta = jnp.sum(mixed * grad.astype(jnp.float32), axis=0, keepdims=True)
    query_back = (query.astype(jnp.float32) * (inverse * scale)).T.astype(jnp.bfloat16)
    grad_back = (grad.astype(jnp.float32) * inverse).T.astype(jnp.bfloat16)

    def back_step(c, grad_query):
        probs = score_buf[c]
        low = probs.astype(jnp.bfloat16)
        grad_probs = jnp.dot(value_rows[c], grad, preferred_element_type=jnp.float32)
        grad_scores = (probs * (grad_probs - delta)).astype(jnp.bfloat16)
        value_sum[c] += jnp.dot(low, grad_back, preferred_element_type=jnp.float32)
        key_sum[c] += jnp.dot(grad_scores, query_back, preferred_element_type=jnp.float32)
        return grad_query + jnp.dot(
            key_ref[c], grad_scores, preferred_element_type=jnp.float32
        )

    grad_query = lax.fori_loop(
        0, chunks, back_step, jnp.zeros((HEAD_DIM, query_len), jnp.float32)
    )
    grad_query_ref[...] = grad_query * (inverse * scale)

    @pl.when(block == pl.num_programs(2) - 1)
    def _():
        def turn(c, carry):
            grad_pair_ref[c, 0] = key_sum[c].T.astype(jnp.bfloat16)
            grad_pair_ref[c, 1] = value_sum[c].T.astype(jnp.bfloat16)
            return carry

        lax.fori_loop(0, chunks, turn, 0)


def attend(query, key_value, grad, own_places, all_places, seq_count, block_len):
    width, row_count = query.shape
    chunks = key_value.shape[0]
    heads = width // HEAD_DIM
    query_len = 512 if block_len % 512 == 0 else block_len
    blocks = block_len // query_len
    column_places = jnp.broadcast_to(
        all_places.reshape(chunks, row_count)[..., None], (chunks, row_count, 128)
    )
    row_places = own_places.reshape(row_count // query_len, 1, query_len)
    one = pl.BlockSpec((HEAD_DIM, query_len), lambda s, h, i: (h, s * blocks + i))
    every = pl.BlockSpec((chunks, HEAD_DIM, block_len), lambda s, h, i: (0, h, s))
    pairs = row_count * chunks * block_len * heads
    return pl.pallas_call(
        attend_kernel,
        grid=(seq_count, heads, blocks),
        in_specs=[
            pl.BlockSpec((1, 1, query_len), lambda s, h, i: (s * blocks + i, 0, 0)),
            pl.BlockSpec((chunks, block_len, 128), lambda s, h, i: (0, s, 0)),
            one,
            every,
            pl.BlockSpec((chunks, HEAD_DIM, block_len), lambda s, h, i: (0, h + heads, s)),
            one,
        ],
        out_specs=[
            one,
            one,
            pl.BlockSpec((chunks, 2, HEAD_DIM, block_len), lambda s, h, i: (0, 0, h, s)),
        ],
        out_shape=[
            jax.ShapeDtypeStruct((width, row_count), jnp.bfloat16),
            jax.ShapeDtypeStruct((width, row_count), jnp.float32),
            jax.ShapeDtypeStruct((chunks, 2, width, row_count), jnp.bfloat16),
        ],
        scratch_shapes=[
            pltpu.VMEM((chunks, block_len, HEAD_DIM), jnp.bfloat16),
            pltpu.VMEM((chunks, block_len, HEAD_DIM), jnp.bfloat16),
            pltpu.VMEM((chunks, block_len, HEAD_DIM), jnp.float32),
            pltpu.VMEM((chunks, block_len, HEAD_DIM), jnp.float32),
            pltpu.VMEM((chunks, block_len, query_len), jnp.float32),
        ],
        compiler_params=pltpu.CompilerParams(vmem_limit_bytes=50 * 2**20),
        cost_estimate=pl.CostEstimate(
            flops=48 * pairs * HEAD_DIM, bytes_accessed=32 * 2**20, transcendentals=pairs
        ),
    )(row_places, column_places, query, key_value, key_value, grad)


def over_tensor(part):
    low = part.astype(jnp.bfloat16)
    count = lax.axis_size("tensor")
    if count != 2:
        return lax.psum(low, "tensor").astype(jnp.float32)
    other = lax.ppermute(low, "tensor", [(0, 1), (1, 0)])
    return low.astype(jnp.float32) + other.astype(jnp.float32)


def gather_chips(shard):
    count = lax.axis_size("dp")
    return jnp.stack(
        [shard]
        + [
            lax.ppermute(shard, "dp", [(i, (i + 2 * step) % count) for i in range(count)])
            for step in range(1, count // 2)
        ]
    )


def gather_cores(parts):
    count = lax.axis_size("dp")
    chips = count // 2
    here = lax.axis_index("dp")
    other = lax.ppermute(parts, "dp", [(i, i ^ 1) for i in range(count)])
    first = here % 2 == 0
    even = jnp.where(first, parts, other)
    odd = jnp.where(first, other, parts)
    both = jnp.stack([even, odd], axis=1)
    ordered = [
        lax.dynamic_index_in_dim(both, (here // 2 - chip) % chips, 0, keepdims=False)
        for chip in range(chips)
    ]
    return jnp.stack(ordered).reshape(count * parts.shape[1], parts.shape[2])


def after(value, earlier):
    return lax.optimization_barrier((value, earlier))[0]


def scatter_core(grads):
    count = lax.axis_size("dp")
    core = lax.axis_index("dp") % 2
    split = grads.astype(jnp.bfloat16).reshape(count // 2, 2, -1, grads.shape[1])
    keep = lax.dynamic_index_in_dim(split, core, 1, keepdims=False)
    send = lax.dynamic_index_in_dim(split, 1 - core, 1, keepdims=False)
    other = lax.ppermute(send, "dp", [(i, i ^ 1) for i in range(count)])
    return (keep.astype(jnp.float32) + other.astype(jnp.float32)).astype(jnp.bfloat16)


def scatter_chips(half):
    count = lax.axis_size("dp")
    chips = count // 2
    chip = lax.axis_index("dp") // 2
    total = lax.dynamic_index_in_dim(half, chip, 0, keepdims=False).astype(jnp.float32)
    for step in range(1, chips):
        send = lax.dynamic_index_in_dim(half, (chip + step) % chips, 0, keepdims=False)
        other = lax.ppermute(
            send, "dp", [(i, (i + 2 * step) % count) for i in range(count)]
        )
        total = total + other.astype(jnp.float32)
    return total.astype(jnp.bfloat16)


def small_gather(vector, axis):
    count = lax.axis_size(axis)
    here = lax.axis_index(axis)
    parts = jnp.stack(
        [vector]
        + [
            lax.ppermute(vector, axis, [(i, (i + step) % count) for i in range(count)])
            for step in range(1, count)
        ]
    )
    return [
        lax.dynamic_index_in_dim(parts, (here - owner) % count, 0, keepdims=False)
        for owner in range(count)
    ]


def small_sum(vector, axis):
    first, *others = small_gather(vector, axis)
    for other in others:
        first = first + other
    return first


def body(
    tokens,
    positions,
    first_gain,
    first_shift,
    second_gain,
    second_shift,
    w_query,
    w_key,
    w_value,
    query_bias,
    key_bias,
    value_bias,
    w_out,
    out_bias,
    w_up,
    up_bias,
    w_down,
    down_bias,
    cotangent,
):
    seq_count, block_len, model_width = tokens.shape
    row_count = seq_count * block_len
    flat_in = tokens.reshape(row_count, model_width).astype(jnp.float32)
    upstream = cotangent.reshape(row_count, model_width)
    ff_part = w_up.shape[1]
    part_width = w_query.shape[1]
    half_rot = ROT_DIM // 2
    f32 = jnp.float32
    low = jnp.bfloat16

    def mm(spec, left, right):
        return jnp.einsum(spec, left, right, preferred_element_type=f32)

    groups = 2 if (part_width // HEAD_DIM) % 2 == 0 else 1
    group_width = part_width // groups

    first_chips = gather_chips(jnp.concatenate([w_query, w_key, w_value, w_out.T], axis=1))
    rest = after(jnp.concatenate([w_up, w_down.T], axis=1), first_chips)
    rest_chips = gather_chips(rest)
    full_first = gather_cores(first_chips)
    places = jnp.stack(small_gather(after(positions, first_chips), "context"))
    full_qkv = full_first[:, : 3 * part_width]
    full_out = full_first[:, 3 * part_width :]
    plain, inv_std = normalize(flat_in)
    normed_one = (plain * first_gain + first_shift).astype(low)
    normed_two = (plain * second_gain + second_shift).astype(low)
    cosine, sine = rotary_tables(positions)
    cosine = cosine.reshape(row_count, half_rot).T
    sine = sine.reshape(row_count, half_rot).T

    qkv_bias = jnp.concatenate([query_bias, key_bias, value_bias])
    qkv = mm("dc,rd->cr", full_qkv, normed_one) + qkv_bias[:, None]
    query = rotate_rows(qkv[:part_width], cosine, sine).astype(low)
    key = rotate_rows(qkv[part_width : 2 * part_width], cosine, sine).astype(low)
    value = qkv[2 * part_width :].astype(low)
    spans = [slice(g * group_width, (g + 1) * group_width) for g in range(groups)]
    pairs = [jnp.concatenate([key[span], value[span]], axis=0) for span in spans]
    key_values = [lax.all_gather(pairs[0], "context", axis=0, tiled=False)]
    for pair in pairs[1:]:
        pair, key_values[-1] = lax.optimization_barrier((pair, key_values[-1]))
        key_values.append(lax.all_gather(pair, "context", axis=0, tiled=False))
    full_rest = gather_cores(after(rest_chips, pairs[0]))
    full_up = full_rest[:, :ff_part]
    full_down = full_rest[:, ff_part:]

    grad_mixed = mm("dc,rd->cr", full_out, upstream).astype(low)
    inner = mm("rd,df->rf", normed_two, full_up) + up_bias
    below = 0.5 * (1.0 + lax.erf(inner * (0.5**0.5)))
    hidden = (inner * below).astype(low)
    slope = below + inner * jnp.exp(-0.5 * inner * inner) * ((2.0 * math.pi) ** -0.5)
    grad_inner = (mm("rd,df->rf", upstream, full_down) * slope).astype(low)
    grad_ff = jnp.concatenate(
        [mm("rd,rf->df", normed_two, grad_inner), mm("rd,rf->df", upstream, hidden)], axis=1
    )
    half_ff = scatter_core(grad_ff)
    back_two = mm("rf,df->rd", grad_inner, full_up)
    out_two = mm("rf,df->rd", hidden, full_down)
    upstream_wide = upstream.astype(f32)

    query, grad_mixed, half_ff, back_two, out_two = lax.optimization_barrier(
        (query, grad_mixed, half_ff, back_two, out_two)
    )
    quarter_ff = scatter_chips(half_ff)
    mixed, grad_query_rot, key_parts, value_parts = [], [], [], []
    for span, key_value in zip(spans, key_values):
        mixed_part, query_part, pair_all = attend(
            query[span], key_value, grad_mixed[span], positions, places, seq_count, block_len
        )
        if key_parts:
            pair_all, key_parts[-1] = lax.optimization_barrier((pair_all, key_parts[-1]))
        pair = lax.psum_scatter(pair_all, "context", scatter_dimension=0, tiled=False)
        mixed.append(mixed_part)
        grad_query_rot.append(query_part)
        key_parts.append(pair[0])
        value_parts.append(pair[1])
    mixed = jnp.concatenate(mixed, axis=0)
    grad_query_rot = jnp.concatenate(grad_query_rot, axis=0)
    summed = over_tensor(mm("cr,dc->rd", mixed, full_out) + out_two)
    grad_out = mm("rd,cr->dc", upstream, mixed)
    quarter_ff, summed, grad_out, value_parts[-1], key_parts[-1] = lax.optimization_barrier(
        (quarter_ff, summed, grad_out, value_parts[-1], key_parts[-1])
    )
    key_part = jnp.concatenate(key_parts, axis=0)
    value_part = jnp.concatenate(value_parts, axis=0)
    own_ff = lax.psum(quarter_ff, "context")
    block_out = (
        (flat_in + summed + out_bias + down_bias)
        .astype(low)
        .reshape(seq_count, block_len, model_width)
    )

    grad_qkv = jnp.concatenate(
        [
            rotate_rows(grad_query_rot, cosine, -sine).astype(low),
            rotate_rows(key_part.astype(f32), cosine, -sine).astype(low),
            value_part,
        ],
        axis=0,
    )
    back_one = mm("cr,dc->rd", grad_qkv, full_qkv)
    tilted = over_tensor(back_one * first_gain + back_two * second_gain)
    grad_late = jnp.concatenate(
        [grad_out, mm("rd,cr->dc", normed_one, grad_qkv)], axis=1
    )
    tilted, quarter_late = lax.optimization_barrier(
        (tilted, scatter_chips(scatter_core(grad_late)))
    )
    first_mean = jnp.mean(tilted, axis=-1, keepdims=True)
    second_mean = jnp.mean(tilted * plain, axis=-1, keepdims=True)
    grad_tokens = (
        upstream_wide + inv_std * (tilted - first_mean - plain * second_mean)
    ).reshape(seq_count, block_len, model_width)

    quarter_late, own_ff = lax.optimization_barrier((quarter_late, own_ff))
    own_late = lax.psum(quarter_late, "context").astype(f32)
    own_ff = own_ff.astype(f32)

    gains = jnp.stack(
        [
            jnp.sum(back_one * plain, axis=0),
            jnp.sum(back_one, axis=0),
            jnp.sum(back_two * plain, axis=0),
            jnp.sum(back_two, axis=0),
        ]
    ).reshape(-1)
    biases = jnp.concatenate(
        [
            jnp.sum(grad_qkv.astype(f32), axis=1),
            jnp.sum(grad_inner.astype(f32), axis=0),
            jnp.sum(upstream_wide, axis=0),
        ]
    )
    vector = jnp.concatenate([gains, biases]).reshape(1, -1)
    vector = small_sum(small_sum(vector, "dp"), "context")
    sum_g = small_sum(vector[:, : gains.shape[0]], "tensor").reshape(4, model_width)
    sum_g1, sum_s1, sum_g2, sum_s2 = sum_g
    sum_b = vector[0, gains.shape[0] :]
    cuts = [part_width, 2 * part_width, 3 * part_width, 3 * part_width + ff_part]
    sum_qb, sum_kb, sum_vb, sum_ub, sum_ob = jnp.split(sum_b, cuts)
    shard_out, shard_query, shard_key, shard_value = jnp.split(own_late, 4, axis=1)
    shard_up = own_ff[:, :ff_part]
    shard_down = own_ff[:, ff_part:].T
    shard_out = shard_out.T
    return (
        block_out,
        grad_tokens,
        sum_g1,
        sum_s1,
        sum_g2,
        sum_s2,
        shard_query,
        shard_key,
        shard_value,
        sum_qb,
        sum_kb,
        sum_vb,
        shard_out,
        sum_ob,
        shard_up,
        sum_ub,
        shard_down,
        sum_ob,
    )


def solution(mesh):
    return jax.shard_map(
        body,
        mesh=mesh,
        in_specs=(
            P("dp", "context", None),
            P("dp", "context"),
            P(),
            P(),
            P(),
            P(),
            P("dp", "tensor"),
            P("dp", "tensor"),
            P("dp", "tensor"),
            P("tensor"),
            P("tensor"),
            P("tensor"),
            P("tensor", "dp"),
            P(),
            P("dp", "tensor"),
            P("tensor"),
            P("tensor", "dp"),
            P(),
            P("dp", "context", None),
        ),
        out_specs=(
            P("dp", "context", None),
            P("dp", "context", None),
            P(),
            P(),
            P(),
            P(),
            P("dp", "tensor"),
            P("dp", "tensor"),
            P("dp", "tensor"),
            P("tensor"),
            P("tensor"),
            P("tensor"),
            P("tensor", "dp"),
            P(),
            P("dp", "tensor"),
            P("tensor"),
            P("tensor", "dp"),
            P(),
        ),
        check_vma=False,
    )
```
